32 devices in a mesh: groups: 2 (over y), row: 4 (over z), col: 2 (over x), chan: 2 (over core).
Axes of the slice: x: 2, y: 2, z: 4, core: 2. Of those that a mesh axis runs over, the one named last changes fastest.
Arguments:
- pair_act: bfloat16 [192, 96, 128], P(('groups', 'row'), 'col'), parts along dimension 0, may hold values from -40 to 40
- res_mask: int32 [192], P('groups'), parts along dimension 0, may hold values 0 or 1
- in_gain: float32 [2, 128], replicated, may hold values from 0.25 to 1.75
- in_bias: float32 [2, 128], replicated, may hold values from -1.5 to 1.5
- w_proj: bfloat16 [2, 4, 128, 128], replicated, may hold values from -0.5 to 0.5
- w_gate: bfloat16 [2, 128, 128], replicated, may hold values from -0.5 to 0.5
- out_gain: float32 [2, 128], replicated, may hold values from 0.25 to 1.75
- out_bias: float32 [2, 128], replicated, may hold values from -1.5 to 1.5
- w_out: bfloat16 [2, 128, 128], replicated, may hold values from -0.5 to 0.5
Outputs:
- pair_out: float32 [192, 96, 128], P(('groups', 'row', 'chan'), 'col'), parts along dimension 0
The draws below stay inside these ranges and needn't reach their ends.
There are 2 independent parts, one for each index of `groups`. The reference program is written for one: setup_inputs(seed, part) draws one part's arguments, and reference() takes and returns one part's arrays. A program takes and returns all parts, laid end to end along the dimension named above; an argument that names none is the same for every part. Nothing has to cross between parts.
All inputs are finite; a program needn't handle non-finite values.
Results may differ from the reference program's by a relative error of at most 0.0015.
Values may be sent and summed in bfloat16 or wider, within the bound.
A program may use at most 128 MiB of HBM per device.

```python
import math
import jax
import jax.numpy as jnp
from jax import lax

C_Z = 128
C_H = 128
N = 96


def draw_pair_act(key, part):
    key = jax.random.fold_in(key, 7)
    key_cell, key_chan, key_noise = jax.random.split(key, 3)
    half_span = 0.5 * math.log(10.0)
    cell_scale = jnp.exp(jax.random.uniform(key_cell, (N, N, 1), jnp.float32, -half_span, half_span))
    chan_scale = jnp.exp(jax.random.uniform(key_chan, (C_Z,), jnp.float32, -half_span, half_span))
    values = jnp.clip(jax.random.normal(key_noise, (N, N, C_Z), jnp.float32), -4.0, 4.0)
    return (cell_scale * chan_scale * values).astype(jnp.bfloat16)


def plant(drawn, key, smallest, largest):
    longest = drawn.shape.index(max(drawn.shape))
    spots = []
    for shift in (0, 1):
        where = [jax.random.randint(jax.random.fold_in(key, axis), (), 0, length) for axis, length in enumerate(drawn.shape)]
        where[longest] = (where[longest] + shift) % drawn.shape[longest]
        spots.append(tuple(where))
    return drawn.at[spots[0]].set(smallest).at[spots[1]].set(largest)


def scatter_about(rng, extent, deviation, limit, kind=jnp.bfloat16):
    values = jax.random.normal(rng, extent, jnp.float32) * deviation
    return jnp.minimum(jnp.maximum(values, -limit), limit).astype(kind)


def setup_inputs(seed: int = 0, part: int = 0) -> dict:
    streams_of = jax.random.split(jax.random.key(seed), 10)
    part_keys = jax.random.split(jax.random.fold_in(streams_of[9], part), 10)
    pair_act = draw_pair_act(jax.random.fold_in(jax.random.fold_in(streams_of[9], part), 71), part)
    res_mask = plant((jax.random.randint(part_keys[1], (N,), 0, 8) < 7).astype(jnp.int32), jax.random.fold_in(part_keys[1], 1), 0, 1)
    in_gain = jnp.clip(1.0 + 0.15 * jax.random.normal(streams_of[2], (2, C_Z), jnp.float32), 0.25, 1.75)
    in_bias = scatter_about(streams_of[3], (2, C_Z), 0.3, 1.5, jnp.float32)
    w_proj = scatter_about(streams_of[4], (2, 4, C_Z, C_H), C_Z ** -0.5, 0.5)
    w_gate = scatter_about(streams_of[5], (2, C_Z, C_Z), C_Z ** -0.5, 0.5)
    out_gain = jnp.clip(1.0 + 0.15 * jax.random.normal(streams_of[6], (2, C_H), jnp.float32), 0.25, 1.75)
    out_bias = scatter_about(streams_of[7], (2, C_H), 0.3, 1.5, jnp.float32)
    w_out = scatter_about(streams_of[8], (2, C_H, C_Z), C_H ** -0.5, 0.5)
    return dict(pair_act=pair_act, res_mask=res_mask, in_gain=in_gain, in_bias=in_bias, w_proj=w_proj, w_gate=w_gate, out_gain=out_gain, out_bias=out_bias, w_out=w_out)


EPSILON = 1e-05

def layer_norm(values, gain_vec, offset, norm_axis):
    average = lax.optimization_barrier(jnp.mean(values, axis=norm_axis, keepdims=True))
    centred = values - average
    variance = lax.optimization_barrier(jnp.mean(centred * centred, axis=norm_axis, keepdims=True))
    return centred * lax.rsqrt(variance + EPSILON) * gain_vec + offset

def reference(pair_act, res_mask, in_gain, in_bias, w_proj, w_gate, out_gain, out_bias, w_out):
    mask_float = res_mask.astype(jnp.float32)
    pair_mask = (mask_float[:, None] * mask_float[None, :])[:, :, None]
    pair_now = pair_act.astype(jnp.float32)
    for layer_no in range(2):
        normed = layer_norm(pair_now, in_gain[layer_no], in_bias[layer_no], 2).astype(jnp.bfloat16)
        flat_rows = normed.reshape(N * N, C_Z)

        def project(which):
            return jnp.dot(flat_rows, w_proj[layer_no, which], preferred_element_type=jnp.float32).reshape(N, N, C_H)
        left_side = (pair_mask * jax.nn.sigmoid(project(0)) * project(1)).astype(jnp.bfloat16)
        right_side = (pair_mask * jax.nn.sigmoid(project(2)) * project(3)).astype(jnp.bfloat16)
        gate_act = jax.nn.sigmoid(jnp.dot(flat_rows, w_gate[layer_no], preferred_element_type=jnp.float32)).reshape(N, N, C_Z)
        left_wide = left_side.astype(jnp.float32)
        right_wide = right_side.astype(jnp.float32)
        if layer_no == 0:
            summed = jnp.einsum('ikc,jkc->ijc', left_wide, right_wide)
        else:
            summed = jnp.einsum('kic,kjc->ijc', left_wide, right_wide)
        triangle = summed.astype(jnp.bfloat16)
        unit_act = layer_norm(triangle.astype(jnp.float32), out_gain[layer_no], out_bias[layer_no], 2).astype(jnp.bfloat16)
        mixed_out = jnp.dot(unit_act.reshape(N * N, C_H), w_out[layer_no], preferred_element_type=jnp.float32).reshape(N, N, C_Z)
        pair_now = pair_now + gate_act * mixed_out
    return pair_now
```

```python
import functools

import jax
import jax.numpy as jnp
from jax import lax
from jax.experimental import pallas as pl
from jax.experimental.pallas import tpu as pltpu
from jax.sharding import PartitionSpec as P

EPSILON = 1e-05


def layer_norm(values, gain_vec, offset, norm_axis):
    average = jnp.mean(values, axis=norm_axis, keepdims=True)
    centred = values - average
    variance = jnp.mean(centred * centred, axis=norm_axis, keepdims=True)
    return centred * lax.rsqrt(variance + EPSILON) * gain_vec + offset


def project_pair(normed, weights, mask_tile):
    projected = jnp.einsum("rsd,wde->wers", normed, weights, preferred_element_type=jnp.float32)
    left_side = (mask_tile * jax.nn.sigmoid(projected[0]) * projected[1]).astype(jnp.bfloat16)
    right_side = (mask_tile * jax.nn.sigmoid(projected[2]) * projected[3]).astype(jnp.bfloat16)
    return (left_side, right_side)


def triangle_core(left_side, right_side, incoming):
    full_left = lax.all_gather(left_side, "col", axis=2, tiled=True)
    if incoming:
        summed = jnp.einsum(
            "cki,ckj->cij", full_left, right_side, preferred_element_type=jnp.float32
        )
    else:
        right_rows = lax.all_to_all(right_side, "col", split_axis=1, concat_axis=2, tiled=True)
        summed = jnp.einsum(
            "cik,cjk->cij", full_left, right_rows, preferred_element_type=jnp.float32
        )
    return summed.astype(jnp.bfloat16)


def finish_layer(update, normed, pair_now, w_gate_layer, gain_vec, offset, w_out_layer):
    gate_act = jax.nn.sigmoid(
        jnp.einsum("rsd,dz->rsz", normed, w_gate_layer, preferred_element_type=jnp.float32)
    )
    unit_act = layer_norm(
        update.astype(jnp.float32), gain_vec[:, None, None], offset[:, None, None], 0
    ).astype(jnp.bfloat16)
    mixed_out = jnp.einsum("ers,ez->rsz", unit_act, w_out_layer, preferred_element_type=jnp.float32)
    return pair_now + gate_act * mixed_out


def local(pair_act, res_mask, in_gain, in_bias, w_proj, w_gate, out_gain, out_bias, w_out):
    tile_rows = pair_act.shape[0]
    tile_cols = pair_act.shape[1]
    core_count = lax.axis_size("chan")
    half_rows = tile_rows // core_count
    width_h = w_proj.shape[3]
    half_width = width_h // core_count
    core_index = lax.axis_index("chan")
    own_start = core_index * half_rows
    mask_float = res_mask.astype(jnp.float32)
    row_start = lax.axis_index("row") * tile_rows
    col_mask = lax.dynamic_slice_in_dim(mask_float, lax.axis_index("col") * tile_cols, tile_cols)
    pair_now = pair_act.astype(jnp.float32)
    row_mask = lax.dynamic_slice_in_dim(mask_float, row_start, tile_rows)
    mask_tile = row_mask[:, None] * col_mask[None, :]
    for layer_no in range(2):
        incoming = layer_no == 1
        gain_vec = out_gain[layer_no]
        offset = out_bias[layer_no]
        w_out_layer = w_out[layer_no]
        if incoming:
            pair_now = lax.all_gather(pair_now, "chan", axis=0, tiled=True)
        normed = layer_norm(pair_now, in_gain[layer_no], in_bias[layer_no], 2).astype(jnp.bfloat16)
        weights = lax.dynamic_slice_in_dim(w_proj[layer_no], core_index * half_width, half_width, 2)
        left_side, right_side = project_pair(normed, weights, mask_tile)
        left_side, right_side = (
            lax.all_to_all(left_side, "row", split_axis=0, concat_axis=1, tiled=True),
            lax.all_to_all(right_side, "row", split_axis=0, concat_axis=1, tiled=True),
        )
        product = triangle_core(left_side, right_side, incoming)
        returned = lax.all_to_all(product, "row", split_axis=1, concat_axis=0, tiled=True)
        update = lax.all_to_all(returned, "chan", split_axis=1, concat_axis=0, tiled=True)
        normed = lax.dynamic_slice_in_dim(normed, own_start, half_rows, 0)
        pair_now = lax.dynamic_slice_in_dim(pair_now, own_start, half_rows, 0)
        pair_now = finish_layer(
            update, normed, pair_now, w_gate[layer_no], gain_vec, offset, w_out_layer
        )
    return pair_now


MESH = pl.DeviceIdType.MESH


def fused_norm(values, gain_vec, offset):
    average = jnp.mean(values, axis=-1, keepdims=True)
    centred = values - average
    variance = jnp.mean(centred * centred, axis=-1, keepdims=True)
    return (centred * lax.rsqrt(variance + EPSILON) * gain_vec + offset).astype(jnp.bfloat16)


def dot_f32(a, b):
    return jnp.dot(a, b, preferred_element_type=jnp.float32)


def fused_kernel(
    sizes, pair_ref, mask_rows_ref, mask_cols_ref, in_gain_ref, in_bias_ref, w_proj_ref, w_gate_ref,
    out_gain_ref, out_bias_ref, w_out_ref, out_ref,
    right_all, left_f32, right_f32, part_f32, part_send, part_recv, left_cut, left_send, left_all,
    left_blk, tri, pair_1, gate,
    right_recv_sem, right_fwd_sem, right_sib_sem, part_send_sem, part_recv_sem, left_send_sem, left_recv_sem,
):
    rows, cols, cores, half, width = sizes
    blocks = rows * cores
    per_col = blocks // cols
    tokens = half * width
    cell = half * half
    z = lax.axis_index("row")
    x = lax.axis_index("col")
    c = lax.axis_index("chan")
    me = z * cores + c
    sib = 1 - c
    channels = pair_ref.shape[-1]

    barrier = pltpu.get_barrier_semaphore()
    for dz in range(rows):
        for dx in range(cols):
            for dc in range(cores):
                if dz or dx or dc:
                    pl.semaphore_signal(
                        barrier, inc=1,
                        device_id={
                            "row": lax.rem(z + dz, rows),
                            "col": lax.rem(x + dx, cols),
                            "chan": lax.rem(c + dc, cores),
                        },
                        device_id_type=MESH,
                    )

    def right_copy(layer, zb, cb, send_sem, device_id):
        return pltpu.make_async_remote_copy(
            src_ref=right_all.at[layer, zb, cb],
            dst_ref=right_all.at[layer, zb, cb],
            send_sem=send_sem,
            recv_sem=right_recv_sem.at[layer, zb, cb],
            device_id=device_id,
            device_id_type=MESH,
        )

    def fwd_right(layer, zb):
        return right_copy(layer, zb, c, right_fwd_sem.at[layer, zb], {"row": z + 1})

    def fwd_left(layer, zb, slot):
        return right_copy(layer, zb, c, right_fwd_sem.at[layer, slot], {"row": z - 1})

    def to_sib(layer, zb):
        return right_copy(layer, zb, c, right_sib_sem.at[layer, zb], {"chan": sib})

    def start_right(layer):
        @pl.when(z + 1 < rows)
        def _():
            fwd_right(layer, z).start()

        @pl.when(z > 0)
        def _():
            fwd_left(layer, z, rows).start()

        to_sib(layer, z).start()

    def relay(layer, s):
        @pl.when(z - s >= 0)
        def _():
            right_copy(layer, z - s, c, right_sib_sem.at[layer, z - s], {"chan": sib}).wait_recv()

            @pl.when(z + 1 < rows)
            def _():
                fwd_right(layer, z - s).start()

            to_sib(layer, z - s).start()

        @pl.when(z + s < rows)
        def _():
            right_copy(layer, z + s, c, right_sib_sem.at[layer, z + s], {"chan": sib}).wait_recv()

            @pl.when(z > 0)
            def _():
                fwd_left(layer, z + s, z + s).start()

            to_sib(layer, z + s).start()

    def finish_right(layer):
        @pl.when(z + 1 < rows)
        def _():
            fwd_right(layer, z).wait_send()

        @pl.when(z > 0)
        def _():
            fwd_left(layer, z, rows).wait_send()

        to_sib(layer, z).wait_send()
        for s in range(1, rows):
            @pl.when(z - s >= 0)
            def _():
                @pl.when(z + 1 < rows)
                def _():
                    fwd_right(layer, z - s).wait_send()

                to_sib(layer, z - s).wait_send()

            @pl.when(z + s < rows)
            def _():
                @pl.when(z > 0)
                def _():
                    fwd_left(layer, z + s, z + s).wait_send()

                to_sib(layer, z + s).wait_send()

    def each_block(layer, work):
        work(z, c)
        right_copy(layer, z, sib, right_sib_sem.at[layer, z], {"chan": sib}).wait_recv()
        work(z, sib)

        def at_distance(s, _):
            relay(layer, s)

            def one(t, _):
                zb = z + s * (2 * (t % 2) - 1)
                cb = (c + t // 2) % 2

                @pl.when((zb >= 0) & (zb < rows))
                def _():
                    @pl.when(t >= 2)
                    def _():
                        right_copy(layer, zb, cb, right_sib_sem.at[layer, zb], {"chan": sib}).wait_recv()

                    work(zb, cb)

                return 0

            lax.fori_loop(0, 4, one, 0)
            return 0

        lax.fori_loop(1, rows, at_distance, 0)

    mask_cols = mask_cols_ref[pl.ds(pl.multiple_of(x * width, 8), width)]
    mask_tile = mask_rows_ref[pl.ds(me * half, half)] * mask_cols[None]

    def gated(normed, layer, which):
        opened = jax.nn.sigmoid(dot_f32(normed, w_proj_ref[layer, which]))
        value = opened * dot_f32(normed, w_proj_ref[layer, which + 1])
        return (mask_tile * value.reshape(half, width, channels)).astype(jnp.bfloat16)

    def finish_layer_here(layer, pair_now):
        unit = fused_norm(
            tri[...].reshape(tokens, channels).astype(jnp.bfloat16).astype(jnp.float32),
            out_gain_ref[pl.ds(layer, 1)], out_bias_ref[pl.ds(layer, 1)],
        )
        return pair_now + gate[...] * dot_f32(unit, w_out_ref[layer])

    pair_0 = pair_ref[pl.ds(c * half, half)].astype(jnp.float32).reshape(tokens, channels)
    normed = fused_norm(pair_0, in_gain_ref[pl.ds(0, 1)], in_bias_ref[pl.ds(0, 1)])
    right_all[0, z, c] = gated(normed, 0, 2)
    pl.semaphore_wait(barrier, blocks * cols - 1)
    start_right(0)
    left_f32[...] = gated(normed, 0, 0).astype(jnp.float32)
    gate[...] = jax.nn.sigmoid(dot_f32(normed, w_gate_ref[0]))

    def part_copy(q, dx, zb_cb):
        return pltpu.make_async_remote_copy(
            src_ref=part_send.at[zb_cb],
            dst_ref=part_recv.at[x, q],
            send_sem=part_send_sem.at[zb_cb],
            recv_sem=part_recv_sem.at[x, q],
            device_id={"col": dx},
            device_id_type=MESH,
        )

    def outgoing(zb, cb):
        b = zb * cores + cb
        right_f32[...] = right_all[0, zb, cb].astype(jnp.float32)

        def one_row(i, _):
            left_row = left_f32[i]
            left_blk[i] = jnp.sum(left_row[None] * right_f32[...], axis=1)
            return 0

        lax.fori_loop(0, half, one_row, 0)
        for i in range(half):
            part_f32[b, i * half:(i + 1) * half] = left_blk[i]

        @pl.when(b // per_col != x)
        def _():
            part_send[b] = part_f32[b].astype(jnp.bfloat16)
            part_copy(b % per_col, b // per_col, b).start()

    each_block(0, outgoing)

    for q in range(per_col):
        total = part_f32[x * per_col + q]
        for d in range(1, cols):
            xs = lax.rem(x + d, cols)
            pltpu.make_async_remote_copy(
                src_ref=part_send.at[0], dst_ref=part_recv.at[xs, q],
                send_sem=part_send_sem.at[0], recv_sem=part_recv_sem.at[xs, q],
                device_id={"col": xs}, device_id_type=MESH,
            ).wait_recv()
            total = total + part_recv[xs, q].astype(jnp.float32)
        for i in range(half):
            tri[i, q * half:(q + 1) * half] = total[i * half:(i + 1) * half]

    pair_1[...] = finish_layer_here(0, pair_0)

    normed = fused_norm(pair_1[...], in_gain_ref[pl.ds(1, 1)], in_bias_ref[pl.ds(1, 1)])
    right_all[1, z, c] = gated(normed, 1, 2)
    start_right(1)
    left_f32[...] = gated(normed, 1, 0).astype(jnp.float32)
    for p in range(per_col):
        for k in range(half):
            left_cut[p, k * half:(k + 1) * half] = left_f32[k, p * half:(p + 1) * half]
        left_send[p] = left_cut[p].astype(jnp.bfloat16)

    def left_copy(p, dx):
        b = x * per_col + p
        return pltpu.make_async_remote_copy(
            src_ref=left_send.at[p],
            dst_ref=left_all.at[me],
            send_sem=left_send_sem.at[p, dx],
            recv_sem=left_recv_sem.at[me],
            device_id={"row": b // cores, "col": dx, "chan": b % cores},
            device_id_type=MESH,
        )

    for p in range(per_col):
        for dx in range(cols):
            is_me = (x * per_col + p == me) & (x == dx)

            @pl.when(jnp.logical_not(is_me))
            def _():
                left_copy(p, dx).start()

            @pl.when(is_me)
            def _():
                left_all[me] = left_send[p]

    gate[...] = jax.nn.sigmoid(dot_f32(normed, w_gate_ref[1]))
    tri[...] = jnp.zeros_like(tri)
    step = 4 if half % 4 == 0 else 1

    def incoming(zb, cb):
        b = zb * cores + cb

        @pl.when(jnp.logical_not((b == me) & (x == me // per_col)))
        def _():
            pltpu.make_async_remote_copy(
                src_ref=left_send.at[0], dst_ref=left_all.at[b],
                send_sem=left_send_sem.at[0, 0], recv_sem=left_recv_sem.at[b],
                device_id={"chan": sib}, device_id_type=MESH,
            ).wait_recv()

        left_cut[0] = left_all[b].astype(jnp.float32)
        right_f32[...] = right_all[1, zb, cb].astype(jnp.float32)
        for i0 in range(0, half, step):
            sums = [tri[i0 + i] for i in range(step)]
            for k in range(half):
                right_row = right_f32[k]
                for i in range(step):
                    at = k * half + i0 + i
                    sums[i] = sums[i] + left_cut[0, at:at + 1] * right_row
            for i in range(step):
                tri[i0 + i] = sums[i]

    each_block(1, incoming)
    out_ref[...] = finish_layer_here(1, pair_1[...]).reshape(half, width, channels)

    finish_right(0)
    finish_right(1)
    for b in range(blocks):
        @pl.when(b // per_col != x)
        def _():
            part_copy(b % per_col, b // per_col, b).wait_send()

    for p in range(per_col):
        for dx in range(cols):
            @pl.when(jnp.logical_not((x * per_col + p == me) & (x == dx)))
            def _():
                left_copy(p, dx).wait_send()


def fused_local(
    sizes, pair_act, res_mask, in_gain, in_bias, w_proj, w_gate, out_gain, out_bias, w_out
):
    rows, cols, cores, half, width = sizes
    blocks = rows * cores
    per_col = blocks // cols
    cell = half * half
    channels = pair_act.shape[-1]
    mask_cols = jnp.broadcast_to(res_mask.astype(jnp.float32)[:, None], (res_mask.shape[0], channels))
    mask_rows = mask_cols[:, None, :]
    f32, bf16, dma = jnp.float32, jnp.bfloat16, pltpu.SemaphoreType.DMA
    return pl.pallas_call(
        functools.partial(fused_kernel, sizes),
        out_shape=jax.ShapeDtypeStruct((half, width, channels), f32),
        in_specs=[pl.BlockSpec(memory_space=pltpu.VMEM)] * 10,
        out_specs=pl.BlockSpec(memory_space=pltpu.VMEM),
        scratch_shapes=[
            pltpu.VMEM((2, rows, cores, half, width, channels), bf16),
            pltpu.VMEM((half, width, channels), f32),
            pltpu.VMEM((half, width, channels), f32),
            pltpu.VMEM((blocks, cell, channels), f32),
            pltpu.VMEM((blocks, cell, channels), bf16),
            pltpu.VMEM((cols, per_col, cell, channels), bf16),
            pltpu.VMEM((per_col, cell, channels), f32),
            pltpu.VMEM((per_col, cell, channels), bf16),
            pltpu.VMEM((blocks, cell, channels), bf16),
            pltpu.VMEM((half, half, channels), f32),
            pltpu.VMEM((half, width, channels), f32),
            pltpu.VMEM((half * width, channels), f32),
            pltpu.VMEM((half * width, channels), f32),
            dma((2, rows, cores)),
            dma((2, rows + 1)),
            dma((2, rows)),
            dma((blocks,)),
            dma((cols, per_col)),
            dma((per_col, cols)),
            dma((blocks,)),
        ],
        compiler_params=pltpu.CompilerParams(
            collective_id=0, has_side_effects=True, vmem_limit_bytes=48 * 1024 * 1024
        ),
    )(pair_act, mask_rows, mask_cols, in_gain, in_bias, w_proj, w_gate, out_gain, out_bias, w_out)


def local_any(
    axis_sizes, pair_act, res_mask, in_gain, in_bias, w_proj, w_gate, out_gain, out_bias, w_out
):
    rows, cols, cores = axis_sizes
    half = pair_act.shape[0] // cores
    width = pair_act.shape[1]
    blocks = rows * cores
    fits = cores == 2 and blocks % cols == 0 and width == half * (blocks // cols)
    fits = fits and width % 16 == 0 and (half * half) % 16 == 0
    fits = fits and blocks * half * width * pair_act.shape[2] <= 1 << 20
    args = (pair_act, res_mask, in_gain, in_bias, w_proj, w_gate, out_gain, out_bias, w_out)
    if fits:
        return fused_local((rows, cols, cores, half, width), *args)
    return local(*args)


def solution(mesh):
    axis_sizes = tuple(mesh.shape[name] for name in ("row", "col", "chan"))
    in_specs = (P(("groups", "row"), "col", None), P("groups"), P(), P(), P(), P(), P(), P(), P())
    out_specs = P(("groups", "row", "chan"), "col", None)
    return jax.shard_map(functools.partial(local_any, axis_sizes), mesh=mesh, in_specs=in_specs, out_specs=out_specs, check_vma=False)
```

```python
import functools

import jax
import jax.numpy as jnp
from jax import lax
from jax.experimental import pallas as pl
from jax.experimental.pallas import tpu as pltpu
from jax.sharding import PartitionSpec as P

EPSILON = 1e-05


def layer_norm(values, gain_vec, offset, norm_axis):
    average = jnp.mean(values, axis=norm_axis, keepdims=True)
    centred = values - average
    variance = jnp.mean(centred * centred, axis=norm_axis, keepdims=True)
    return centred * lax.rsqrt(variance + EPSILON) * gain_vec + offset


def project_pair(normed, weights, mask_tile):
    projected = jnp.einsum("rsd,wde->wers", normed, weights, preferred_element_type=jnp.float32)
    left_side = (mask_tile * jax.nn.sigmoid(projected[0]) * projected[1]).astype(jnp.bfloat16)
    right_side = (mask_tile * jax.nn.sigmoid(projected[2]) * projected[3]).astype(jnp.bfloat16)
    return (left_side, right_side)


def triangle_core(left_side, right_side, incoming):
    full_left = lax.all_gather(left_side, "col", axis=2, tiled=True)
    if incoming:
        summed = jnp.einsum(
            "cki,ckj->cij", full_left, right_side, preferred_element_type=jnp.float32
        )
    else:
        right_rows = lax.all_to_all(right_side, "col", split_axis=1, concat_axis=2, tiled=True)
        summed = jnp.einsum(
            "cik,cjk->cij", full_left, right_rows, preferred_element_type=jnp.float32
        )
    return summed.astype(jnp.bfloat16)


def finish_layer(update, normed, pair_now, w_gate_layer, gain_vec, offset, w_out_layer):
    gate_act = jax.nn.sigmoid(
        jnp.einsum("rsd,dz->rsz", normed, w_gate_layer, preferred_element_type=jnp.float32)
    )
    unit_act = layer_norm(
        update.astype(jnp.float32), gain_vec[:, None, None], offset[:, None, None], 0
    ).astype(jnp.bfloat16)
    mixed_out = jnp.einsum("ers,ez->rsz", unit_act, w_out_layer, preferred_element_type=jnp.float32)
    return pair_now + gate_act * mixed_out


def local(pair_act, res_mask, in_gain, in_bias, w_proj, w_gate, out_gain, out_bias, w_out):
    tile_rows = pair_act.shape[0]
    tile_cols = pair_act.shape[1]
    core_count = lax.axis_size("chan")
    half_rows = tile_rows // core_count
    width_h = w_proj.shape[3]
    half_width = width_h // core_count
    core_index = lax.axis_index("chan")
    own_start = core_index * half_rows
    mask_float = res_mask.astype(jnp.float32)
    row_start = lax.axis_index("row") * tile_rows
    col_mask = lax.dynamic_slice_in_dim(mask_float, lax.axis_index("col") * tile_cols, tile_cols)
    pair_now = pair_act.astype(jnp.float32)
    row_mask = lax.dynamic_slice_in_dim(mask_float, row_start, tile_rows)
    mask_tile = row_mask[:, None] * col_mask[None, :]
    for layer_no in range(2):
        incoming = layer_no == 1
        gain_vec = out_gain[layer_no]
        offset = out_bias[layer_no]
        w_out_layer = w_out[layer_no]
        if incoming:
            pair_now = lax.all_gather(pair_now, "chan", axis=0, tiled=True)
        normed = layer_norm(pair_now, in_gain[layer_no], in_bias[layer_no], 2).astype(jnp.bfloat16)
        weights = lax.dynamic_slice_in_dim(w_proj[layer_no], core_index * half_width, half_width, 2)
        left_side, right_side = project_pair(normed, weights, mask_tile)
        left_side, right_side = (
            lax.all_to_all(left_side, "row", split_axis=0, concat_axis=1, tiled=True),
            lax.all_to_all(right_side, "row", split_axis=0, concat_axis=1, tiled=True),
        )
        product = triangle_core(left_side, right_side, incoming)
        returned = lax.all_to_all(product, "row", split_axis=1, concat_axis=0, tiled=True)
        update = lax.all_to_all(returned, "chan", split_axis=1, concat_axis=0, tiled=True)
        normed = lax.dynamic_slice_in_dim(normed, own_start, half_rows, 0)
        pair_now = lax.dynamic_slice_in_dim(pair_now, own_start, half_rows, 0)
        pair_now = finish_layer(
            update, normed, pair_now, w_gate[layer_no], gain_vec, offset, w_out_layer
        )
    return pair_now


MESH = pl.DeviceIdType.MESH


def fused_norm(values, gain_vec, offset):
    average = jnp.mean(values, axis=-1, keepdims=True)
    centred = values - average
    variance = jnp.mean(centred * centred, axis=-1, keepdims=True)
    return (centred * lax.rsqrt(variance + EPSILON) * gain_vec + offset).astype(jnp.bfloat16)


def dot_f32(a, b):
    return jnp.dot(a, b, preferred_element_type=jnp.float32)


def fused_kernel(
    sizes, mask_row_ref, mask_ref, pair_hbm, in_gain_ref, in_bias_ref, w_proj_hbm, w_gate_hbm,
    out_gain_ref, out_bias_ref, w_out_hbm, out_ref,
    right_all, left_f32, right_f32, part_f32, part_send, part_recv, left_cut, left_send, left_peer,
    left_all, left_blk, tri, pair_1, gate, pair_ref, w_proj_ref, w_gate_ref, w_out_ref,
    right_recv_sem, right_fwd_sem, right_sib_sem, part_send_sem, part_recv_sem,
    left_send_sem, left_recv_sem, left_relay_sem, peer_send_sem, peer_recv_sem, load_sem,
):
    rows, cols, cores, half, width = sizes
    blocks = rows * cores
    per_col = blocks // cols
    tokens = half * width
    cell = half * half
    z = lax.axis_index("row")
    x = lax.axis_index("col")
    c = lax.axis_index("chan")
    me = z * cores + c
    sib = 1 - c
    channels = pair_ref.shape[-1]

    barrier = pltpu.get_barrier_semaphore()
    for device_id in ({"chan": sib}, {"col": 1 - x}):
        pl.semaphore_signal(barrier, inc=1, device_id=device_id, device_id_type=MESH)

    @pl.when(z > 0)
    def _():
        pl.semaphore_signal(barrier, inc=1, device_id={"row": z - 1}, device_id_type=MESH)

    @pl.when(z + 1 < rows)
    def _():
        pl.semaphore_signal(barrier, inc=1, device_id={"row": z + 1}, device_id_type=MESH)

    loads = [
        pltpu.make_async_copy(pair_hbm.at[pl.ds(c * half, half)], pair_ref, load_sem.at[0]),
        pltpu.make_async_copy(w_proj_hbm, w_proj_ref, load_sem.at[1]),
        pltpu.make_async_copy(w_gate_hbm, w_gate_ref, load_sem.at[2]),
        pltpu.make_async_copy(w_out_hbm, w_out_ref, load_sem.at[3]),
    ]
    for load in loads:
        load.start()

    def right_copy(layer, zb, cb, send_sem, device_id):
        return pltpu.make_async_remote_copy(
            src_ref=right_all.at[layer, zb, cb],
            dst_ref=right_all.at[layer, zb, cb],
            send_sem=send_sem,
            recv_sem=right_recv_sem.at[layer, zb, cb],
            device_id=device_id,
            device_id_type=MESH,
        )

    def fwd_right(layer, zb):
        return right_copy(layer, zb, c, right_fwd_sem.at[layer, zb], {"row": z + 1})

    def fwd_left(layer, zb, slot):
        return right_copy(layer, zb, c, right_fwd_sem.at[layer, slot], {"row": z - 1})

    def to_sib(layer, zb):
        return right_copy(layer, zb, c, right_sib_sem.at[layer, zb], {"chan": sib})

    def start_right(layer):
        @pl.when(z + 1 < rows)
        def _():
            fwd_right(layer, z).start()

        @pl.when(z > 0)
        def _():
            fwd_left(layer, z, rows).start()

        to_sib(layer, z).start()

    def relay(layer, s):
        @pl.when(z - s >= 0)
        def _():
            right_copy(layer, z - s, c, right_sib_sem.at[layer, z - s], {"chan": sib}).wait_recv()

            @pl.when(z + 1 < rows)
            def _():
                fwd_right(layer, z - s).start()

            to_sib(layer, z - s).start()

        @pl.when(z + s < rows)
        def _():
            right_copy(layer, z + s, c, right_sib_sem.at[layer, z + s], {"chan": sib}).wait_recv()

            @pl.when(z > 0)
            def _():
                fwd_left(layer, z + s, z + s).start()

            to_sib(layer, z + s).start()

    def finish_right(layer):
        @pl.when(z + 1 < rows)
        def _():
            fwd_right(layer, z).wait_send()

        @pl.when(z > 0)
        def _():
            fwd_left(layer, z, rows).wait_send()

        to_sib(layer, z).wait_send()
        for s in range(1, rows):
            @pl.when(z - s >= 0)
            def _():
                @pl.when(z + 1 < rows)
                def _():
                    fwd_right(layer, z - s).wait_send()

                to_sib(layer, z - s).wait_send()

            @pl.when(z + s < rows)
            def _():
                @pl.when(z > 0)
                def _():
                    fwd_left(layer, z + s, z + s).wait_send()

                to_sib(layer, z + s).wait_send()

    def each_block(layer, work, after_relay=None):
        work(z, c)
        right_copy(layer, z, sib, right_sib_sem.at[layer, z], {"chan": sib}).wait_recv()
        work(z, sib)

        def at_distance(s, _):
            relay(layer, s)
            if after_relay is not None:
                after_relay(s)

            def one(t, _):
                zb = z + s * (2 * (t % 2) - 1)
                cb = (c + t // 2) % 2

                @pl.when((zb >= 0) & (zb < rows))
                def _():
                    @pl.when(t >= 2)
                    def _():
                        right_copy(layer, zb, cb, right_sib_sem.at[layer, zb], {"chan": sib}).wait_recv()

                    work(zb, cb)

                return 0

            lax.fori_loop(0, 4, one, 0)
            return 0

        lax.fori_loop(1, rows, at_distance, 0)

    tokens_all = mask_ref.shape[1]
    lane = lax.broadcasted_iota(jnp.int32, (width, tokens_all), 1)
    here = lax.broadcasted_iota(jnp.int32, (width, tokens_all), 0) + x * width
    mask_cols = jnp.sum(
        jnp.where(lane == here, mask_ref[...].astype(jnp.float32), 0.0), axis=1, keepdims=True
    )
    mask_cols = jnp.broadcast_to(mask_cols, (width, channels))
    mask_tile = jnp.stack(
        [mask_cols * mask_row_ref[0, me * half + r].astype(jnp.float32) for r in range(half)]
    )

    def gated(normed, layer, which):
        opened = jax.nn.sigmoid(dot_f32(normed, w_proj_ref[layer, which]))
        value = opened * dot_f32(normed, w_proj_ref[layer, which + 1])
        return (mask_tile * value.reshape(half, width, channels)).astype(jnp.bfloat16)

    def finish_layer_here(layer, pair_now):
        unit = fused_norm(
            tri[...].reshape(tokens, channels).astype(jnp.bfloat16).astype(jnp.float32),
            out_gain_ref[pl.ds(layer, 1)], out_bias_ref[pl.ds(layer, 1)],
        )
        return pair_now + gate[...] * dot_f32(unit, w_out_ref[layer])

    loads[0].wait()
    pair_0 = pair_ref[...].astype(jnp.float32).reshape(tokens, channels)
    normed = fused_norm(pair_0, in_gain_ref[pl.ds(0, 1)], in_bias_ref[pl.ds(0, 1)])
    loads[1].wait()
    right_all[0, z, c] = gated(normed, 0, 2)
    pl.semaphore_wait(barrier, 2 + jnp.minimum(z, 1) + jnp.minimum(rows - 1 - z, 1))

    start_right(0)
    left_f32[...] = gated(normed, 0, 0).astype(jnp.float32)
    loads[2].wait()
    gate[...] = jax.nn.sigmoid(dot_f32(normed, w_gate_ref[0]))
    loads[3].wait()

    def part_copy(q, dx, zb_cb):
        return pltpu.make_async_remote_copy(
            src_ref=part_send.at[zb_cb],
            dst_ref=part_recv.at[x, q],
            send_sem=part_send_sem.at[zb_cb],
            recv_sem=part_recv_sem.at[x, q],
            device_id={"col": dx},
            device_id_type=MESH,
        )

    def outgoing(zb, cb):
        b = zb * cores + cb
        right_f32[...] = right_all[0, zb, cb].astype(jnp.float32)

        def one_row(i, _):
            left_row = left_f32[i]
            left_blk[i] = jnp.sum(left_row[None] * right_f32[...], axis=1)
            return 0

        lax.fori_loop(0, half, one_row, 0)
        for i in range(half):
            part_f32[b, i * half:(i + 1) * half] = left_blk[i]

        @pl.when(b // per_col != x)
        def _():
            part_send[b] = part_f32[b].astype(jnp.bfloat16)
            part_copy(b % per_col, b // per_col, b).start()

    each_block(0, outgoing)

    for q in range(per_col):
        total = part_f32[x * per_col + q]
        for d in range(1, cols):
            xs = lax.rem(x + d, cols)
            pltpu.make_async_remote_copy(
                src_ref=part_send.at[0], dst_ref=part_recv.at[xs, q],
                send_sem=part_send_sem.at[0], recv_sem=part_recv_sem.at[xs, q],
                device_id={"col": xs}, device_id_type=MESH,
            ).wait_recv()
            total = total + part_recv[xs, q].astype(jnp.float32)
        for i in range(half):
            tri[i, q * half:(q + 1) * half] = total[i * half:(i + 1) * half]

    pair_1[...] = finish_layer_here(0, pair_0)

    normed = fused_norm(pair_1[...], in_gain_ref[pl.ds(1, 1)], in_bias_ref[pl.ds(1, 1)])
    right_all[1, z, c] = gated(normed, 1, 2)
    start_right(1)
    left_f32[...] = gated(normed, 1, 0).astype(jnp.float32)
    for p in range(per_col):
        for k in range(half):
            left_cut[p, k * half:(k + 1) * half] = left_f32[k, p * half:(p + 1) * half]
        left_send[p] = left_cut[p].astype(jnp.bfloat16)

    carries = c == x
    peer = pltpu.make_async_remote_copy(
        src_ref=left_send, dst_ref=left_peer, send_sem=peer_send_sem, recv_sem=peer_recv_sem,
        device_id={"col": 1 - x}, device_id_type=MESH,
    )

    def left_copy(source, p, b):
        return pltpu.make_async_remote_copy(
            src_ref=source.at[p],
            dst_ref=left_all.at[me],
            send_sem=left_send_sem.at[b],
            recv_sem=left_recv_sem.at[me],
            device_id={"row": b // cores, "chan": b % cores},
            device_id_type=MESH,
        )

    def left_relay(b):
        return pltpu.make_async_remote_copy(
            src_ref=left_all.at[b],
            dst_ref=left_all.at[b],
            send_sem=left_relay_sem.at[b],
            recv_sem=left_recv_sem.at[b],
            device_id={"col": 1 - x},
            device_id_type=MESH,
        )

    def send_pieces(source, column):
        def one(p, _):
            b = column * per_col + p

            @pl.when(b != me)
            def _():
                left_copy(source, p, b).start()

            @pl.when(b == me)
            def _():
                left_all[me] = source[p]
                left_relay(me).start()

            return 0

        lax.fori_loop(0, per_col, one, 0)

    def pass_left(zb):
        left_relay(zb * cores + x).wait_recv()
        left_relay(zb * cores + x).start()

    def pass_left_at(s):
        @pl.when(z - s >= 0)
        def _():
            pass_left(z - s)

        @pl.when(z + s < rows)
        def _():
            pass_left(z + s)

    @pl.when(carries)
    def _():
        send_pieces(left_send, x)
        peer.wait_recv()
        send_pieces(left_peer, 1 - x)

    @pl.when(jnp.logical_not(carries))
    def _():
        peer.start()

    gate[...] = jax.nn.sigmoid(dot_f32(normed, w_gate_ref[1]))
    tri[...] = jnp.zeros_like(tri)
    step = 4 if half % 4 == 0 else 1

    def incoming(zb, cb):
        b = zb * cores + cb

        @pl.when(cb != x)
        def _():
            left_relay(b).wait_recv()

        left_cut[0] = left_all[b].astype(jnp.float32)
        right_f32[...] = right_all[1, zb, cb].astype(jnp.float32)
        for i0 in range(0, half, step):
            sums = [tri[i0 + i] for i in range(step)]
            for k in range(half):
                right_row = right_f32[k]
                for i in range(step):
                    at = k * half + i0 + i
                    sums[i] = sums[i] + left_cut[0, at:at + 1] * right_row
            for i in range(step):
                tri[i0 + i] = sums[i]

    @pl.when(jnp.logical_not(carries))
    def _():
        pass_left(z)

    each_block(1, incoming, pass_left_at)
    out_ref[...] = finish_layer_here(1, pair_1[...]).reshape(half, width, channels)

    finish_right(0)
    finish_right(1)
    for b in range(blocks):
        @pl.when(b // per_col != x)
        def _():
            part_copy(b % per_col, b // per_col, b).wait_send()

    for zb in range(rows):
        left_relay(zb * cores + x).wait_send()

    @pl.when(carries)
    def _():
        for b in range(blocks):
            @pl.when(b != me)
            def _():
                left_copy(left_send, 0, b).wait_send()

    @pl.when(jnp.logical_not(carries))
    def _():
        peer.wait_send()


def fused_local(
    sizes, pair_act, res_mask, in_gain, in_bias, w_proj, w_gate, out_gain, out_bias, w_out
):
    rows, cols, cores, half, width = sizes
    blocks = rows * cores
    per_col = blocks // cols
    cell = half * half
    channels = pair_act.shape[-1]
    mask_row = res_mask.reshape(1, res_mask.shape[0])
    f32, bf16, dma = jnp.float32, jnp.bfloat16, pltpu.SemaphoreType.DMA
    vmem, hbm = pltpu.VMEM, pltpu.HBM
    return pl.pallas_call(
        functools.partial(fused_kernel, sizes),
        out_shape=jax.ShapeDtypeStruct((half, width, channels), f32),
        in_specs=[
            pl.BlockSpec(memory_space=space)
            for space in (pltpu.SMEM, vmem, hbm, vmem, vmem, hbm, hbm, vmem, vmem, hbm)
        ],
        out_specs=pl.BlockSpec(memory_space=pltpu.VMEM),
        scratch_shapes=[
            pltpu.VMEM((2, rows, cores, half, width, channels), bf16),
            pltpu.VMEM((half, width, channels), f32),
            pltpu.VMEM((half, width, channels), f32),
            pltpu.VMEM((blocks, cell, channels), f32),
            pltpu.VMEM((blocks, cell, channels), bf16),
            pltpu.VMEM((cols, per_col, cell, channels), bf16),
            pltpu.VMEM((per_col, cell, channels), f32),
            pltpu.VMEM((per_col, cell, channels), bf16),
            pltpu.VMEM((per_col, cell, channels), bf16),
            pltpu.VMEM((blocks, cell, channels), bf16),
            pltpu.VMEM((half, half, channels), f32),
            pltpu.VMEM((half, width, channels), f32),
            pltpu.VMEM((half * width, channels), f32),
            pltpu.VMEM((half * width, channels), f32),
            pltpu.VMEM((half, width, channels), bf16),
            pltpu.VMEM(w_proj.shape, bf16),
            pltpu.VMEM(w_gate.shape, bf16),
            pltpu.VMEM(w_out.shape, bf16),
            dma((2, rows, cores)),
            dma((2, rows + 1)),
            dma((2, rows)),
            dma((blocks,)),
            dma((cols, per_col)),
            dma((blocks,)),
            dma((blocks,)),
            dma((blocks,)),
            dma(()),
            dma(()),
            dma((4,)),
        ],
        compiler_params=pltpu.CompilerParams(
            collective_id=0, has_side_effects=True, vmem_limit_bytes=48 * 1024 * 1024
        ),
    )(mask_row, mask_row, pair_act, in_gain, in_bias, w_proj, w_gate, out_gain, out_bias, w_out)


def local_any(
    axis_sizes, pair_act, res_mask, in_gain, in_bias, w_proj, w_gate, out_gain, out_bias, w_out
):
    rows, cols, cores = axis_sizes
    half = pair_act.shape[0] // cores
    width = pair_act.shape[1]
    blocks = rows * cores
    fits = cores == 2 and cols == 2 and blocks % cols == 0 and width == half * (blocks // cols)
    fits = fits and width % 16 == 0 and (half * half) % 16 == 0
    fits = fits and blocks * half * width * pair_act.shape[2] <= 1 << 20
    args = (pair_act, res_mask, in_gain, in_bias, w_proj, w_gate, out_gain, out_bias, w_out)
    if fits:
        return fused_local((rows, cols, cores, half, width), *args)
    return local(*args)


def solution(mesh):
    axis_sizes = tuple(mesh.shape[name] for name in ("row", "col", "chan"))
    in_specs = (P(("groups", "row"), "col", None), P("groups"), P(), P(), P(), P(), P(), P(), P())
    out_specs = P(("groups", "row", "chan"), "col", None)
    return jax.shard_map(functools.partial(local_any, axis_sizes), mesh=mesh, in_specs=in_specs, out_specs=out_specs, check_vma=False)
```

```python
import functools

import jax
import jax.numpy as jnp
from jax import lax
from jax.experimental import pallas as pl
from jax.experimental.pallas import tpu as pltpu
from jax.sharding import PartitionSpec as P

EPSILON = 1e-05


def layer_norm(values, gain_vec, offset, norm_axis):
    average = jnp.mean(values, axis=norm_axis, keepdims=True)
    centred = values - average
    variance = jnp.mean(centred * centred, axis=norm_axis, keepdims=True)
    return centred * lax.rsqrt(variance + EPSILON) * gain_vec + offset


def project_pair(normed, weights, mask_tile):
    projected = jnp.einsum("rsd,wde->wers", normed, weights, preferred_element_type=jnp.float32)
    left_side = (mask_tile * jax.nn.sigmoid(projected[0]) * projected[1]).astype(jnp.bfloat16)
    right_side = (mask_tile * jax.nn.sigmoid(projected[2]) * projected[3]).astype(jnp.bfloat16)
    return (left_side, right_side)


def triangle_core(left_side, right_side, incoming):
    full_left = lax.all_gather(left_side, "col", axis=2, tiled=True)
    if incoming:
        summed = jnp.einsum(
            "cki,ckj->cij", full_left, right_side, preferred_element_type=jnp.float32
        )
    else:
        right_rows = lax.all_to_all(right_side, "col", split_axis=1, concat_axis=2, tiled=True)
        summed = jnp.einsum(
            "cik,cjk->cij", full_left, right_rows, preferred_element_type=jnp.float32
        )
    return summed.astype(jnp.bfloat16)


def finish_layer(update, normed, pair_now, w_gate_layer, gain_vec, offset, w_out_layer):
    gate_act = jax.nn.sigmoid(
        jnp.einsum("rsd,dz->rsz", normed, w_gate_layer, preferred_element_type=jnp.float32)
    )
    unit_act = layer_norm(
        update.astype(jnp.float32), gain_vec[:, None, None], offset[:, None, None], 0
    ).astype(jnp.bfloat16)
    mixed_out = jnp.einsum("ers,ez->rsz", unit_act, w_out_layer, preferred_element_type=jnp.float32)
    return pair_now + gate_act * mixed_out


def local(pair_act, res_mask, in_gain, in_bias, w_proj, w_gate, out_gain, out_bias, w_out):
    tile_rows = pair_act.shape[0]
    tile_cols = pair_act.shape[1]
    core_count = lax.axis_size("chan")
    half_rows = tile_rows // core_count
    width_h = w_proj.shape[3]
    half_width = width_h // core_count
    core_index = lax.axis_index("chan")
    own_start = core_index * half_rows
    mask_float = res_mask.astype(jnp.float32)
    row_start = lax.axis_index("row") * tile_rows
    col_mask = lax.dynamic_slice_in_dim(mask_float, lax.axis_index("col") * tile_cols, tile_cols)
    pair_now = pair_act.astype(jnp.float32)
    row_mask = lax.dynamic_slice_in_dim(mask_float, row_start, tile_rows)
    mask_tile = row_mask[:, None] * col_mask[None, :]
    for layer_no in range(2):
        incoming = layer_no == 1
        gain_vec = out_gain[layer_no]
        offset = out_bias[layer_no]
        w_out_layer = w_out[layer_no]
        if incoming:
            pair_now = lax.all_gather(pair_now, "chan", axis=0, tiled=True)
        normed = layer_norm(pair_now, in_gain[layer_no], in_bias[layer_no], 2).astype(jnp.bfloat16)
        weights = lax.dynamic_slice_in_dim(w_proj[layer_no], core_index * half_width, half_width, 2)
        left_side, right_side = project_pair(normed, weights, mask_tile)
        left_side, right_side = (
            lax.all_to_all(left_side, "row", split_axis=0, concat_axis=1, tiled=True),
            lax.all_to_all(right_side, "row", split_axis=0, concat_axis=1, tiled=True),
        )
        product = triangle_core(left_side, right_side, incoming)
        returned = lax.all_to_all(product, "row", split_axis=1, concat_axis=0, tiled=True)
        update = lax.all_to_all(returned, "chan", split_axis=1, concat_axis=0, tiled=True)
        normed = lax.dynamic_slice_in_dim(normed, own_start, half_rows, 0)
        pair_now = lax.dynamic_slice_in_dim(pair_now, own_start, half_rows, 0)
        pair_now = finish_layer(
            update, normed, pair_now, w_gate[layer_no], gain_vec, offset, w_out_layer
        )
    return pair_now


MESH = pl.DeviceIdType.MESH


def fused_norm(values, gain_vec, offset):
    average = jnp.mean(values, axis=-1, keepdims=True)
    centred = values - average
    variance = jnp.mean(centred * centred, axis=-1, keepdims=True)
    return (centred * lax.rsqrt(variance + EPSILON) * gain_vec + offset).astype(jnp.bfloat16)


def dot_f32(a, b):
    return jnp.dot(a, b, preferred_element_type=jnp.float32)


def right_chunks(half):
    return 2 if half % 2 == 0 else 1


def fused_kernel(
    sizes, mask_row_ref, mask_ref, pair_hbm, in_gain_ref, in_bias_ref, w_proj_hbm, w_gate_hbm,
    out_gain_ref, out_bias_ref, w_out_hbm, out_ref,
    right_all, left_f32, right_f32, part_f32, part_send, part_recv, left_cut, left_send, left_peer,
    left_all, left_blk, tri, pair_1, gate, pair_ref, w_proj_ref, w_gate_ref, w_out_ref,
    right_recv_sem, right_fwd_sem, right_sib_sem, part_send_sem, part_recv_sem,
    left_send_sem, left_recv_sem, left_relay_sem, peer_send_sem, peer_recv_sem, load_sem,
):
    rows, cols, cores, half, width = sizes
    blocks = rows * cores
    per_col = blocks // cols
    tokens = half * width
    chunks = right_chunks(half)
    cell = half * half
    z = lax.axis_index("row")
    x = lax.axis_index("col")
    c = lax.axis_index("chan")
    me = z * cores + c
    sib = 1 - c
    channels = pair_ref.shape[-1]

    barrier = pltpu.get_barrier_semaphore()
    for device_id in ({"chan": sib}, {"col": 1 - x}):
        pl.semaphore_signal(barrier, inc=1, device_id=device_id, device_id_type=MESH)

    @pl.when(z > 0)
    def _():
        pl.semaphore_signal(barrier, inc=1, device_id={"row": z - 1}, device_id_type=MESH)

    @pl.when(z + 1 < rows)
    def _():
        pl.semaphore_signal(barrier, inc=1, device_id={"row": z + 1}, device_id_type=MESH)

    loads = [
        pltpu.make_async_copy(pair_hbm.at[pl.ds(c * half, half)], pair_ref, load_sem.at[0]),
        pltpu.make_async_copy(w_proj_hbm, w_proj_ref, load_sem.at[1]),
        pltpu.make_async_copy(w_gate_hbm, w_gate_ref, load_sem.at[2]),
        pltpu.make_async_copy(w_out_hbm, w_out_ref, load_sem.at[3]),
    ]
    for load in loads:
        load.start()

    chunk = half // chunks

    def right_copy(layer, zb, cb, h, send_sem, device_id):
        part = right_all.at[layer, zb, cb, pl.ds(h * chunk, chunk)]
        return pltpu.make_async_remote_copy(
            src_ref=part,
            dst_ref=part,
            send_sem=send_sem,
            recv_sem=right_recv_sem.at[layer, zb, cb, h],
            device_id=device_id,
            device_id_type=MESH,
        )

    def fwd_right(layer, zb, h):
        return right_copy(layer, zb, c, h, right_fwd_sem.at[layer, zb, h], {"row": z + 1})

    def fwd_left(layer, zb, slot, h):
        return right_copy(layer, zb, c, h, right_fwd_sem.at[layer, slot, h], {"row": z - 1})

    def to_sib(layer, zb, h):
        return right_copy(layer, zb, c, h, right_sib_sem.at[layer, zb, h], {"chan": sib})

    def wait_right(layer, zb, cb):
        for h in range(chunks):
            right_copy(layer, zb, cb, h, right_sib_sem.at[layer, zb, h], {"chan": sib}).wait_recv()

    def start_right(layer):
        for h in range(chunks):
            @pl.when(z + 1 < rows)
            def _():
                fwd_right(layer, z, h).start()

            @pl.when(z > 0)
            def _():
                fwd_left(layer, z, rows, h).start()

        for h in range(chunks):
            to_sib(layer, z, h).start()

    def relay(layer, s):
        for h in range(chunks):
            @pl.when(z - s >= 0)
            def _():
                to_sib(layer, z - s, h).wait_recv()

                @pl.when(z + 1 < rows)
                def _():
                    fwd_right(layer, z - s, h).start()

                to_sib(layer, z - s, h).start()

            @pl.when(z + s < rows)
            def _():
                to_sib(layer, z + s, h).wait_recv()

                @pl.when(z > 0)
                def _():
                    fwd_left(layer, z + s, z + s, h).start()

                to_sib(layer, z + s, h).start()

    def finish_right(layer):
        def one(h, _):
            @pl.when(z + 1 < rows)
            def _():
                fwd_right(layer, z, h).wait_send()

            @pl.when(z > 0)
            def _():
                fwd_left(layer, z, rows, h).wait_send()

            to_sib(layer, z, h).wait_send()
            for s in range(1, rows):
                @pl.when(z - s >= 0)
                def _():
                    @pl.when(z + 1 < rows)
                    def _():
                        fwd_right(layer, z - s, h).wait_send()

                    to_sib(layer, z - s, h).wait_send()

                @pl.when(z + s < rows)
                def _():
                    @pl.when(z > 0)
                    def _():
                        fwd_left(layer, z + s, z + s, h).wait_send()

                    to_sib(layer, z + s, h).wait_send()

            return 0

        lax.fori_loop(0, chunks, one, 0)

    def each_block(layer, work, after_relay=None):
        work(z, c)

        def at_distance(s, _):
            relay(layer, s)
            if after_relay is not None:
                after_relay(s)

            def one(t, _):
                own = t // 2
                far = s - 1 + own
                zb = z + far * (1 - 2 * (t % 2))
                cb = (c + 1 - own) % 2

                @pl.when((zb >= 0) & (zb < rows) & ((far > 0) | (t % 2 == 0)))
                def _():
                    @pl.when(own == 0)
                    def _():
                        wait_right(layer, zb, cb)

                    work(zb, cb)

                return 0

            lax.fori_loop(0, 4, one, 0)
            return 0

        lax.fori_loop(1, rows + 1, at_distance, 0)

    tokens_all = mask_ref.shape[1]
    lane = lax.broadcasted_iota(jnp.int32, (width, tokens_all), 1)
    here = lax.broadcasted_iota(jnp.int32, (width, tokens_all), 0) + x * width
    mask_cols = jnp.sum(
        jnp.where(lane == here, mask_ref[...].astype(jnp.float32), 0.0), axis=1, keepdims=True
    )
    mask_cols = jnp.broadcast_to(mask_cols, (width, channels))
    mask_tile = jnp.stack(
        [mask_cols * mask_row_ref[0, me * half + r].astype(jnp.float32) for r in range(half)]
    )

    def gated(normed, layer, which):
        opened = jax.nn.sigmoid(dot_f32(normed, w_proj_ref[layer, which]))
        value = opened * dot_f32(normed, w_proj_ref[layer, which + 1])
        return (mask_tile * value.reshape(half, width, channels)).astype(jnp.bfloat16)

    def finish_layer_here(layer, pair_now):
        unit = fused_norm(
            tri[...].reshape(tokens, channels).astype(jnp.bfloat16).astype(jnp.float32),
            out_gain_ref[pl.ds(layer, 1)], out_bias_ref[pl.ds(layer, 1)],
        )
        return pair_now + gate[...] * dot_f32(unit, w_out_ref[layer])

    loads[0].wait()
    pair_0 = pair_ref[...].astype(jnp.float32).reshape(tokens, channels)
    normed = fused_norm(pair_0, in_gain_ref[pl.ds(0, 1)], in_bias_ref[pl.ds(0, 1)])
    loads[1].wait()
    right_all[0, z, c] = gated(normed, 0, 2)
    pl.semaphore_wait(barrier, 2 + jnp.minimum(z, 1) + jnp.minimum(rows - 1 - z, 1))

    start_right(0)
    left_f32[...] = gated(normed, 0, 0).astype(jnp.float32)
    loads[2].wait()
    gate[...] = jax.nn.sigmoid(dot_f32(normed, w_gate_ref[0]))
    loads[3].wait()

    def part_copy(q, dx, zb_cb):
        return pltpu.make_async_remote_copy(
            src_ref=part_send.at[zb_cb],
            dst_ref=part_recv.at[x, q],
            send_sem=part_send_sem.at[zb_cb],
            recv_sem=part_recv_sem.at[x, q],
            device_id={"col": dx},
            device_id_type=MESH,
        )

    def outgoing(zb, cb):
        b = zb * cores + cb
        right_f32[...] = right_all[0, zb, cb].astype(jnp.float32)

        def one_row(i, _):
            left_row = left_f32[i]
            left_blk[i] = jnp.sum(left_row[None] * right_f32[...], axis=1)
            return 0

        lax.fori_loop(0, half, one_row, 0)
        for i in range(half):
            part_f32[b, i * half:(i + 1) * half] = left_blk[i]

        @pl.when(b // per_col != x)
        def _():
            part_send[b] = part_f32[b].astype(jnp.bfloat16)
            part_copy(b % per_col, b // per_col, b).start()

    each_block(0, outgoing)

    for q in range(per_col):
        total = part_f32[x * per_col + q]
        for d in range(1, cols):
            xs = lax.rem(x + d, cols)
            pltpu.make_async_remote_copy(
                src_ref=part_send.at[0], dst_ref=part_recv.at[xs, q],
                send_sem=part_send_sem.at[0], recv_sem=part_recv_sem.at[xs, q],
                device_id={"col": xs}, device_id_type=MESH,
            ).wait_recv()
            total = total + part_recv[xs, q].astype(jnp.float32)
        for i in range(half):
            tri[i, q * half:(q + 1) * half] = total[i * half:(i + 1) * half]

    pair_1[...] = finish_layer_here(0, pair_0)

    normed = fused_norm(pair_1[...], in_gain_ref[pl.ds(1, 1)], in_bias_ref[pl.ds(1, 1)])
    right_all[1, z, c] = gated(normed, 1, 2)
    start_right(1)
    left_f32[...] = gated(normed, 1, 0).astype(jnp.float32)
    for p in range(per_col):
        for k in range(half):
            left_cut[p, k * half:(k + 1) * half] = left_f32[k, p * half:(p + 1) * half]
        left_send[p] = left_cut[p].astype(jnp.bfloat16)

    carries = c == x
    peer = pltpu.make_async_remote_copy(
        src_ref=left_send, dst_ref=left_peer, send_sem=peer_send_sem, recv_sem=peer_recv_sem,
        device_id={"col": 1 - x}, device_id_type=MESH,
    )

    def left_copy(source, p, b):
        return pltpu.make_async_remote_copy(
            src_ref=source.at[p],
            dst_ref=left_all.at[me],
            send_sem=left_send_sem.at[b],
            recv_sem=left_recv_sem.at[me],
            device_id={"row": b // cores, "chan": b % cores},
            device_id_type=MESH,
        )

    def left_relay(b):
        return pltpu.make_async_remote_copy(
            src_ref=left_all.at[b],
            dst_ref=left_all.at[b],
            send_sem=left_relay_sem.at[b],
            recv_sem=left_recv_sem.at[b],
            device_id={"col": 1 - x},
            device_id_type=MESH,
        )

    def send_pieces(source, column):
        def one(p, _):
            b = column * per_col + p

            @pl.when(b != me)
            def _():
                left_copy(source, p, b).start()

            @pl.when(b == me)
            def _():
                left_all[me] = source[p]
                left_relay(me).start()

            return 0

        lax.fori_loop(0, per_col, one, 0)

    def pass_left(zb):
        left_relay(zb * cores + x).wait_recv()
        left_relay(zb * cores + x).start()

    def pass_left_at(s):
        @pl.when(z - s >= 0)
        def _():
            pass_left(z - s)

        @pl.when(z + s < rows)
        def _():
            pass_left(z + s)

    @pl.when(carries)
    def _():
        send_pieces(left_send, x)
        peer.wait_recv()
        send_pieces(left_peer, 1 - x)

    @pl.when(jnp.logical_not(carries))
    def _():
        peer.start()

    gate[...] = jax.nn.sigmoid(dot_f32(normed, w_gate_ref[1]))
    tri[...] = jnp.zeros_like(tri)
    step = 4 if half % 4 == 0 else 1

    def incoming(zb, cb):
        b = zb * cores + cb

        @pl.when(cb != x)
        def _():
            left_relay(b).wait_recv()

        left_cut[0] = left_all[b].astype(jnp.float32)
        right_f32[...] = right_all[1, zb, cb].astype(jnp.float32)
        for i0 in range(0, half, step):
            sums = [tri[i0 + i] for i in range(step)]
            for k in range(half):
                right_row = right_f32[k]
                for i in range(step):
                    at = k * half + i0 + i
                    sums[i] = sums[i] + left_cut[0, at:at + 1] * right_row
            for i in range(step):
                tri[i0 + i] = sums[i]

    @pl.when(jnp.logical_not(carries))
    def _():
        pass_left(z)

    each_block(1, incoming, pass_left_at)
    out_ref[...] = finish_layer_here(1, pair_1[...]).reshape(half, width, channels)

    finish_right(0)
    finish_right(1)
    for b in range(blocks):
        @pl.when(b // per_col != x)
        def _():
            part_copy(b % per_col, b // per_col, b).wait_send()

    for zb in range(rows):
        left_relay(zb * cores + x).wait_send()

    @pl.when(carries)
    def _():
        for b in range(blocks):
            @pl.when(b != me)
            def _():
                left_copy(left_send, 0, b).wait_send()

    @pl.when(jnp.logical_not(carries))
    def _():
        peer.wait_send()


def fused_local(
    sizes, pair_act, res_mask, in_gain, in_bias, w_proj, w_gate, out_gain, out_bias, w_out
):
    rows, cols, cores, half, width = sizes
    blocks = rows * cores
    per_col = blocks // cols
    cell = half * half
    channels = pair_act.shape[-1]
    mask_row = res_mask.reshape(1, res_mask.shape[0])
    chunks = right_chunks(half)
    f32, bf16, dma = jnp.float32, jnp.bfloat16, pltpu.SemaphoreType.DMA
    vmem, hbm = pltpu.VMEM, pltpu.HBM
    return pl.pallas_call(
        functools.partial(fused_kernel, sizes),
        out_shape=jax.ShapeDtypeStruct((half, width, channels), f32),
        in_specs=[
            pl.BlockSpec(memory_space=space)
            for space in (pltpu.SMEM, vmem, hbm, vmem, vmem, hbm, hbm, vmem, vmem, hbm)
        ],
        out_specs=pl.BlockSpec(memory_space=pltpu.VMEM),
        scratch_shapes=[
            pltpu.VMEM((2, rows, cores, half, width, channels), bf16),
            pltpu.VMEM((half, width, channels), f32),
            pltpu.VMEM((half, width, channels), f32),
            pltpu.VMEM((blocks, cell, channels), f32),
            pltpu.VMEM((blocks, cell, channels), bf16),
            pltpu.VMEM((cols, per_col, cell, channels), bf16),
            pltpu.VMEM((per_col, cell, channels), f32),
            pltpu.VMEM((per_col, cell, channels), bf16),
            pltpu.VMEM((per_col, cell, channels), bf16),
            pltpu.VMEM((blocks, cell, channels), bf16),
            pltpu.VMEM((half, half, channels), f32),
            pltpu.VMEM((half, width, channels), f32),
            pltpu.VMEM((half * width, channels), f32),
            pltpu.VMEM((half * width, channels), f32),
            pltpu.VMEM((half, width, channels), bf16),
            pltpu.VMEM(w_proj.shape, bf16),
            pltpu.VMEM(w_gate.shape, bf16),
            pltpu.VMEM(w_out.shape, bf16),
            dma((2, rows, cores, chunks)),
            dma((2, rows + 1, chunks)),
            dma((2, rows, chunks)),
            dma((blocks,)),
            dma((cols, per_col)),
            dma((blocks,)),
            dma((blocks,)),
            dma((blocks,)),
            dma(()),
            dma(()),
            dma((4,)),
        ],
        compiler_params=pltpu.CompilerParams(
            collective_id=0, has_side_effects=True, vmem_limit_bytes=64 * 1024 * 1024
        ),
    )(mask_row, mask_row, pair_act, in_gain, in_bias, w_proj, w_gate, out_gain, out_bias, w_out)


def local_any(
    axis_sizes, pair_act, res_mask, in_gain, in_bias, w_proj, w_gate, out_gain, out_bias, w_out
):
    rows, cols, cores = axis_sizes
    half = pair_act.shape[0] // cores
    width = pair_act.shape[1]
    blocks = rows * cores
    fits = cores == 2 and cols == 2 and blocks % cols == 0 and width == half * (blocks // cols)
    fits = fits and width % 16 == 0 and (half * half) % 16 == 0
    fits = fits and blocks * half * width * pair_act.shape[2] <= 1 << 20
    args = (pair_act, res_mask, in_gain, in_bias, w_proj, w_gate, out_gain, out_bias, w_out)
    if fits:
        return fused_local((rows, cols, cores, half, width), *args)
    return local(*args)


def solution(mesh):
    axis_sizes = tuple(mesh.shape[name] for name in ("row", "col", "chan"))
    in_specs = (P(("groups", "row"), "col", None), P("groups"), P(), P(), P(), P(), P(), P(), P())
    out_specs = P(("groups", "row", "chan"), "col", None)
    return jax.shard_map(functools.partial(local_any, axis_sizes), mesh=mesh, in_specs=in_specs, out_specs=out_specs, check_vma=False)
```

```python
import functools

import jax
import jax.numpy as jnp
from jax import lax
from jax.experimental import pallas as pl
from jax.experimental.pallas import tpu as pltpu
from jax.sharding import PartitionSpec as P

EPSILON = 1e-05


def layer_norm(values, gain_vec, offset, norm_axis):
    average = jnp.mean(values, axis=norm_axis, keepdims=True)
    centred = values - average
    variance = jnp.mean(centred * centred, axis=norm_axis, keepdims=True)
    return centred * lax.rsqrt(variance + EPSILON) * gain_vec + offset


def project_pair(normed, weights, mask_tile):
    projected = jnp.einsum("rsd,wde->wers", normed, weights, preferred_element_type=jnp.float32)
    left_side = (mask_tile * jax.nn.sigmoid(projected[0]) * projected[1]).astype(jnp.bfloat16)
    right_side = (mask_tile * jax.nn.sigmoid(projected[2]) * projected[3]).astype(jnp.bfloat16)
    return (left_side, right_side)


def triangle_core(left_side, right_side, incoming):
    full_left = lax.all_gather(left_side, "col", axis=2, tiled=True)
    if incoming:
        summed = jnp.einsum(
            "cki,ckj->cij", full_left, right_side, preferred_element_type=jnp.float32
        )
    else:
        right_rows = lax.all_to_all(right_side, "col", split_axis=1, concat_axis=2, tiled=True)
        summed = jnp.einsum(
            "cik,cjk->cij", full_left, right_rows, preferred_element_type=jnp.float32
        )
    return summed.astype(jnp.bfloat16)


def finish_layer(update, normed, pair_now, w_gate_layer, gain_vec, offset, w_out_layer):
    gate_act = jax.nn.sigmoid(
        jnp.einsum("rsd,dz->rsz", normed, w_gate_layer, preferred_element_type=jnp.float32)
    )
    unit_act = layer_norm(
        update.astype(jnp.float32), gain_vec[:, None, None], offset[:, None, None], 0
    ).astype(jnp.bfloat16)
    mixed_out = jnp.einsum("ers,ez->rsz", unit_act, w_out_layer, preferred_element_type=jnp.float32)
    return pair_now + gate_act * mixed_out


def local(pair_act, res_mask, in_gain, in_bias, w_proj, w_gate, out_gain, out_bias, w_out):
    tile_rows = pair_act.shape[0]
    tile_cols = pair_act.shape[1]
    core_count = lax.axis_size("chan")
    half_rows = tile_rows // core_count
    width_h = w_proj.shape[3]
    half_width = width_h // core_count
    core_index = lax.axis_index("chan")
    own_start = core_index * half_rows
    mask_float = res_mask.astype(jnp.float32)
    row_start = lax.axis_index("row") * tile_rows
    col_mask = lax.dynamic_slice_in_dim(mask_float, lax.axis_index("col") * tile_cols, tile_cols)
    pair_now = pair_act.astype(jnp.float32)
    row_mask = lax.dynamic_slice_in_dim(mask_float, row_start, tile_rows)
    mask_tile = row_mask[:, None] * col_mask[None, :]
    for layer_no in range(2):
        incoming = layer_no == 1
        gain_vec = out_gain[layer_no]
        offset = out_bias[layer_no]
        w_out_layer = w_out[layer_no]
        if incoming:
            pair_now = lax.all_gather(pair_now, "chan", axis=0, tiled=True)
        normed = layer_norm(pair_now, in_gain[layer_no], in_bias[layer_no], 2).astype(jnp.bfloat16)
        weights = lax.dynamic_slice_in_dim(w_proj[layer_no], core_index * half_width, half_width, 2)
        left_side, right_side = project_pair(normed, weights, mask_tile)
        left_side, right_side = (
            lax.all_to_all(left_side, "row", split_axis=0, concat_axis=1, tiled=True),
            lax.all_to_all(right_side, "row", split_axis=0, concat_axis=1, tiled=True),
        )
        product = triangle_core(left_side, right_side, incoming)
        returned = lax.all_to_all(product, "row", split_axis=1, concat_axis=0, tiled=True)
        update = lax.all_to_all(returned, "chan", split_axis=1, concat_axis=0, tiled=True)
        normed = lax.dynamic_slice_in_dim(normed, own_start, half_rows, 0)
        pair_now = lax.dynamic_slice_in_dim(pair_now, own_start, half_rows, 0)
        pair_now = finish_layer(
            update, normed, pair_now, w_gate[layer_no], gain_vec, offset, w_out_layer
        )
    return pair_now


MESH = pl.DeviceIdType.MESH


def fused_norm(values, gain_vec, offset):
    average = jnp.mean(values, axis=-1, keepdims=True)
    centred = values - average
    variance = jnp.mean(centred * centred, axis=-1, keepdims=True)
    return (centred * lax.rsqrt(variance + EPSILON) * gain_vec + offset).astype(jnp.bfloat16)


def dot_f32(a, b):
    return jnp.dot(a, b, preferred_element_type=jnp.float32)


def right_chunks(half):
    return 3 if half % 3 == 0 else 1


def fused_kernel(
    sizes, mask_row_ref, mask_hbm, pair_hbm, in_gain_hbm, in_bias_hbm, w_proj_hbm, w_gate_hbm,
    out_gain_hbm, out_bias_hbm, w_out_hbm, out_ref,
    right_all, left_f32, right_f32, part_f32, part_send, part_recv, left_cut, left_send, left_peer,
    left_all, left_blk, tri, pair_1, gate, pair_ref, w_proj_ref, w_gate_ref, w_out_ref,
    mask_ref, in_gain_ref, in_bias_ref, out_gain_ref, out_bias_ref,
    right_recv_sem, right_fwd_sem, right_sib_sem, part_send_sem, part_recv_sem,
    left_send_sem, left_recv_sem, left_relay_sem, peer_send_sem, peer_recv_sem, load_sem,
):
    rows, cols, cores, half, width = sizes
    blocks = rows * cores
    per_col = blocks // cols
    tokens = half * width
    chunks = right_chunks(half)
    cell = half * half
    z = lax.axis_index("row")
    x = lax.axis_index("col")
    c = lax.axis_index("chan")
    me = z * cores + c
    sib = 1 - c
    channels = pair_ref.shape[-1]

    barrier = pltpu.get_barrier_semaphore()
    for device_id in ({"chan": sib}, {"col": 1 - x}):
        pl.semaphore_signal(barrier, inc=1, device_id=device_id, device_id_type=MESH)

    @pl.when(z > 0)
    def _():
        pl.semaphore_signal(barrier, inc=1, device_id={"row": z - 1}, device_id_type=MESH)

    @pl.when(z + 1 < rows)
    def _():
        pl.semaphore_signal(barrier, inc=1, device_id={"row": z + 1}, device_id_type=MESH)

    loads = [
        pltpu.make_async_copy(pair_hbm.at[pl.ds(c * half, half)], pair_ref, load_sem.at[0]),
        pltpu.make_async_copy(w_proj_hbm, w_proj_ref, load_sem.at[1]),
        pltpu.make_async_copy(w_gate_hbm, w_gate_ref, load_sem.at[2]),
        pltpu.make_async_copy(w_out_hbm, w_out_ref, load_sem.at[3]),
        pltpu.make_async_copy(in_gain_hbm, in_gain_ref, load_sem.at[4]),
        pltpu.make_async_copy(in_bias_hbm, in_bias_ref, load_sem.at[5]),
        pltpu.make_async_copy(mask_hbm, mask_ref, load_sem.at[6]),
        pltpu.make_async_copy(out_gain_hbm, out_gain_ref, load_sem.at[7]),
        pltpu.make_async_copy(out_bias_hbm, out_bias_ref, load_sem.at[8]),
    ]
    for load in loads:
        load.start()

    chunk = half // chunks

    def right_copy(layer, zb, cb, h, send_sem, device_id):
        part = right_all.at[layer, zb, cb, pl.ds(h * chunk, chunk)]
        return pltpu.make_async_remote_copy(
            src_ref=part,
            dst_ref=part,
            send_sem=send_sem,
            recv_sem=right_recv_sem.at[layer, zb, cb, h],
            device_id=device_id,
            device_id_type=MESH,
        )

    def fwd_right(layer, zb, h):
        return right_copy(layer, zb, c, h, right_fwd_sem.at[layer, zb, h], {"row": z + 1})

    def fwd_left(layer, zb, slot, h):
        return right_copy(layer, zb, c, h, right_fwd_sem.at[layer, slot, h], {"row": z - 1})

    def to_sib(layer, zb, h):
        return right_copy(layer, zb, c, h, right_sib_sem.at[layer, zb, h], {"chan": sib})

    def wait_right(layer, zb, cb):
        for h in range(chunks):
            right_copy(layer, zb, cb, h, right_sib_sem.at[layer, zb, h], {"chan": sib}).wait_recv()

    def start_right(layer):
        for h in range(chunks):
            @pl.when(z + 1 < rows)
            def _():
                fwd_right(layer, z, h).start()

            @pl.when(z > 0)
            def _():
                fwd_left(layer, z, rows, h).start()

        for h in range(chunks):
            to_sib(layer, z, h).start()

    def relay(layer, s):
        for h in range(chunks):
            @pl.when(z - s >= 0)
            def _():
                to_sib(layer, z - s, h).wait_recv()

                @pl.when(z + 1 < rows)
                def _():
                    fwd_right(layer, z - s, h).start()

                to_sib(layer, z - s, h).start()

            @pl.when(z + s < rows)
            def _():
                to_sib(layer, z + s, h).wait_recv()

                @pl.when(z > 0)
                def _():
                    fwd_left(layer, z + s, z + s, h).start()

                to_sib(layer, z + s, h).start()

    def finish_right(layer):
        def one(h, _):
            @pl.when(z + 1 < rows)
            def _():
                fwd_right(layer, z, h).wait_send()

            @pl.when(z > 0)
            def _():
                fwd_left(layer, z, rows, h).wait_send()

            to_sib(layer, z, h).wait_send()
            for s in range(1, rows):
                @pl.when(z - s >= 0)
                def _():
                    @pl.when(z + 1 < rows)
                    def _():
                        fwd_right(layer, z - s, h).wait_send()

                    to_sib(layer, z - s, h).wait_send()

                @pl.when(z + s < rows)
                def _():
                    @pl.when(z > 0)
                    def _():
                        fwd_left(layer, z + s, z + s, h).wait_send()

                    to_sib(layer, z + s, h).wait_send()

            return 0

        lax.fori_loop(0, chunks, one, 0)

    def each_block(layer, work, after_relay=None):
        work(z, c)

        def at_distance(s, _):
            relay(layer, s)
            if after_relay is not None:
                after_relay(s)

            def one(t, _):
                own = t // 2
                far = s - 1 + own
                zb = z + far * (1 - 2 * (t % 2))
                cb = (c + 1 - own) % 2

                @pl.when((zb >= 0) & (zb < rows) & ((far > 0) | (t % 2 == 0)))
                def _():
                    @pl.when(own == 0)
                    def _():
                        wait_right(layer, zb, cb)

                    work(zb, cb)

                return 0

            lax.fori_loop(0, 4, one, 0)
            return 0

        lax.fori_loop(1, rows + 1, at_distance, 0)

    tokens_all = mask_ref.shape[1]
    loads[6].wait()
    lane = lax.broadcasted_iota(jnp.int32, (width, tokens_all), 1)
    here = lax.broadcasted_iota(jnp.int32, (width, tokens_all), 0) + x * width
    mask_cols = jnp.sum(
        jnp.where(lane == here, mask_ref[...].astype(jnp.float32), 0.0), axis=1, keepdims=True
    )
    mask_cols = jnp.broadcast_to(mask_cols, (width, channels))
    mask_tile = jnp.stack(
        [mask_cols * mask_row_ref[0, me * half + r].astype(jnp.float32) for r in range(half)]
    )

    def gated(normed, layer, which):
        opened = jax.nn.sigmoid(dot_f32(normed, w_proj_ref[layer, which]))
        value = opened * dot_f32(normed, w_proj_ref[layer, which + 1])
        return (mask_tile * value.reshape(half, width, channels)).astype(jnp.bfloat16)

    def finish_layer_here(layer, pair_now):
        unit = fused_norm(
            tri[...].reshape(tokens, channels).astype(jnp.bfloat16).astype(jnp.float32),
            out_gain_ref[pl.ds(layer, 1)], out_bias_ref[pl.ds(layer, 1)],
        )
        return pair_now + gate[...] * dot_f32(unit, w_out_ref[layer])

    for n in (0, 4, 5):
        loads[n].wait()
    pair_0 = pair_ref[...].astype(jnp.float32).reshape(tokens, channels)
    normed = fused_norm(pair_0, in_gain_ref[pl.ds(0, 1)], in_bias_ref[pl.ds(0, 1)])
    loads[1].wait()
    right_all[0, z, c] = gated(normed, 0, 2)
    pl.semaphore_wait(barrier, 2 + jnp.minimum(z, 1) + jnp.minimum(rows - 1 - z, 1))

    start_right(0)
    left_f32[...] = gated(normed, 0, 0).astype(jnp.float32)
    loads[2].wait()
    gate[...] = jax.nn.sigmoid(dot_f32(normed, w_gate_ref[0]))
    for n in (3, 7, 8):
        loads[n].wait()

    def part_copy(q, dx, zb_cb):
        return pltpu.make_async_remote_copy(
            src_ref=part_send.at[zb_cb],
            dst_ref=part_recv.at[x, q],
            send_sem=part_send_sem.at[zb_cb],
            recv_sem=part_recv_sem.at[x, q],
            device_id={"col": dx},
            device_id_type=MESH,
        )

    def outgoing(zb, cb):
        b = zb * cores + cb
        right_f32[...] = right_all[0, zb, cb].astype(jnp.float32)

        def one_row(i, _):
            left_row = left_f32[i]
            left_blk[i] = jnp.sum(left_row[None] * right_f32[...], axis=1)
            return 0

        lax.fori_loop(0, half, one_row, 0)
        for i in range(half):
            part_f32[b, i * half:(i + 1) * half] = left_blk[i]

        @pl.when(b // per_col != x)
        def _():
            part_send[b] = part_f32[b].astype(jnp.bfloat16)
            part_copy(b % per_col, b // per_col, b).start()

    each_block(0, outgoing)

    for q in range(per_col):
        total = part_f32[x * per_col + q]
        for d in range(1, cols):
            xs = lax.rem(x + d, cols)
            pltpu.make_async_remote_copy(
                src_ref=part_send.at[0], dst_ref=part_recv.at[xs, q],
                send_sem=part_send_sem.at[0], recv_sem=part_recv_sem.at[xs, q],
                device_id={"col": xs}, device_id_type=MESH,
            ).wait_recv()
            total = total + part_recv[xs, q].astype(jnp.float32)
        for i in range(half):
            tri[i, q * half:(q + 1) * half] = total[i * half:(i + 1) * half]

    pair_1[...] = finish_layer_here(0, pair_0)

    normed = fused_norm(pair_1[...], in_gain_ref[pl.ds(1, 1)], in_bias_ref[pl.ds(1, 1)])
    right_all[1, z, c] = gated(normed, 1, 2)
    start_right(1)
    left_f32[...] = gated(normed, 1, 0).astype(jnp.float32)
    for p in range(per_col):
        for k in range(half):
            left_cut[p, k * half:(k + 1) * half] = left_f32[k, p * half:(p + 1) * half]
        left_send[p] = left_cut[p].astype(jnp.bfloat16)

    carries = c == x
    peer = pltpu.make_async_remote_copy(
        src_ref=left_send, dst_ref=left_peer, send_sem=peer_send_sem, recv_sem=peer_recv_sem,
        device_id={"col": 1 - x}, device_id_type=MESH,
    )

    def left_copy(source, p, b):
        return pltpu.make_async_remote_copy(
            src_ref=source.at[p],
            dst_ref=left_all.at[me],
            send_sem=left_send_sem.at[b],
            recv_sem=left_recv_sem.at[me],
            device_id={"row": b // cores, "chan": b % cores},
            device_id_type=MESH,
        )

    def left_relay(b):
        return pltpu.make_async_remote_copy(
            src_ref=left_all.at[b],
            dst_ref=left_all.at[b],
            send_sem=left_relay_sem.at[b],
            recv_sem=left_recv_sem.at[b],
            device_id={"col": 1 - x},
            device_id_type=MESH,
        )

    def send_pieces(source, column):
        def one(p, _):
            b = column * per_col + p

            @pl.when(b != me)
            def _():
                left_copy(source, p, b).start()

            @pl.when(b == me)
            def _():
                left_all[me] = source[p]
                left_relay(me).start()

            return 0

        lax.fori_loop(0, per_col, one, 0)

    def pass_left(zb):
        left_relay(zb * cores + x).wait_recv()
        left_relay(zb * cores + x).start()

    def pass_left_at(s):
        @pl.when(z - s >= 0)
        def _():
            pass_left(z - s)

        @pl.when(z + s < rows)
        def _():
            pass_left(z + s)

    @pl.when(carries)
    def _():
        send_pieces(left_send, x)
        peer.wait_recv()
        send_pieces(left_peer, 1 - x)

    @pl.when(jnp.logical_not(carries))
    def _():
        peer.start()

    gate[...] = jax.nn.sigmoid(dot_f32(normed, w_gate_ref[1]))
    tri[...] = jnp.zeros_like(tri)
    step = 6 if half % 6 == 0 else 1

    def incoming(zb, cb):
        b = zb * cores + cb

        @pl.when(cb != x)
        def _():
            left_relay(b).wait_recv()

        left_cut[0] = left_all[b].astype(jnp.float32)
        right_f32[...] = right_all[1, zb, cb].astype(jnp.float32)
        for i0 in range(0, half, step):
            sums = [tri[i0 + i] for i in range(step)]
            for k in range(half):
                right_row = right_f32[k]
                for i in range(step):
                    at = k * half + i0 + i
                    sums[i] = sums[i] + left_cut[0, at:at + 1] * right_row
            for i in range(step):
                tri[i0 + i] = sums[i]

    @pl.when(jnp.logical_not(carries))
    def _():
        pass_left(z)

    each_block(1, incoming, pass_left_at)
    out_ref[...] = finish_layer_here(1, pair_1[...]).reshape(half, width, channels)

    finish_right(0)
    finish_right(1)
    for b in range(blocks):
        @pl.when(b // per_col != x)
        def _():
            part_copy(b % per_col, b // per_col, b).wait_send()

    for zb in range(rows):
        left_relay(zb * cores + x).wait_send()

    @pl.when(carries)
    def _():
        for b in range(blocks):
            @pl.when(b != me)
            def _():
                left_copy(left_send, 0, b).wait_send()

    @pl.when(jnp.logical_not(carries))
    def _():
        peer.wait_send()


def fused_local(
    sizes, pair_act, res_mask, in_gain, in_bias, w_proj, w_gate, out_gain, out_bias, w_out
):
    rows, cols, cores, half, width = sizes
    blocks = rows * cores
    per_col = blocks // cols
    cell = half * half
    channels = pair_act.shape[-1]
    mask_row = res_mask.reshape(1, res_mask.shape[0])
    chunks = right_chunks(half)
    f32, bf16, dma = jnp.float32, jnp.bfloat16, pltpu.SemaphoreType.DMA
    vmem, hbm = pltpu.VMEM, pltpu.HBM
    return pl.pallas_call(
        functools.partial(fused_kernel, sizes),
        out_shape=jax.ShapeDtypeStruct((half, width, channels), f32),
        in_specs=[
            pl.BlockSpec(memory_space=space)
            for space in (pltpu.SMEM,) + (hbm,) * 9
        ],
        out_specs=pl.BlockSpec(memory_space=pltpu.VMEM),
        scratch_shapes=[
            pltpu.VMEM((2, rows, cores, half, width, channels), bf16),
            pltpu.VMEM((half, width, channels), f32),
            pltpu.VMEM((half, width, channels), f32),
            pltpu.VMEM((blocks, cell, channels), f32),
            pltpu.VMEM((blocks, cell, channels), bf16),
            pltpu.VMEM((cols, per_col, cell, channels), bf16),
            pltpu.VMEM((per_col, cell, channels), f32),
            pltpu.VMEM((per_col, cell, channels), bf16),
            pltpu.VMEM((per_col, cell, channels), bf16),
            pltpu.VMEM((blocks, cell, channels), bf16),
            pltpu.VMEM((half, half, channels), f32),
            pltpu.VMEM((half, width, channels), f32),
            pltpu.VMEM((half * width, channels), f32),
            pltpu.VMEM((half * width, channels), f32),
            pltpu.VMEM((half, width, channels), bf16),
            pltpu.VMEM(w_proj.shape, bf16),
            pltpu.VMEM(w_gate.shape, bf16),
            pltpu.VMEM(w_out.shape, bf16),
            pltpu.VMEM(mask_row.shape, jnp.int32),
            pltpu.VMEM(in_gain.shape, f32),
            pltpu.VMEM(in_gain.shape, f32),
            pltpu.VMEM(in_gain.shape, f32),
            pltpu.VMEM(in_gain.shape, f32),
            dma((2, rows, cores, chunks)),
            dma((2, rows + 1, chunks)),
            dma((2, rows, chunks)),
            dma((blocks,)),
            dma((cols, per_col)),
            dma((blocks,)),
            dma((blocks,)),
            dma((blocks,)),
            dma(()),
            dma(()),
            dma((9,)),
        ],
        compiler_params=pltpu.CompilerParams(
            collective_id=0, has_side_effects=True, vmem_limit_bytes=64 * 1024 * 1024
        ),
    )(mask_row, mask_row, pair_act, in_gain, in_bias, w_proj, w_gate, out_gain, out_bias, w_out)


def local_any(
    axis_sizes, pair_act, res_mask, in_gain, in_bias, w_proj, w_gate, out_gain, out_bias, w_out
):
    rows, cols, cores = axis_sizes
    half = pair_act.shape[0] // cores
    width = pair_act.shape[1]
    blocks = rows * cores
    fits = cores == 2 and cols == 2 and blocks % cols == 0 and width == half * (blocks // cols)
    fits = fits and width % 16 == 0 and (half * half) % 16 == 0
    fits = fits and blocks * half * width * pair_act.shape[2] <= 1 << 20
    args = (pair_act, res_mask, in_gain, in_bias, w_proj, w_gate, out_gain, out_bias, w_out)
    if fits:
        return fused_local((rows, cols, cores, half, width), *args)
    return local(*args)


def solution(mesh):
    axis_sizes = tuple(mesh.shape[name] for name in ("row", "col", "chan"))
    in_specs = (P(("groups", "row"), "col", None), P("groups"), P(), P(), P(), P(), P(), P(), P())
    out_specs = P(("groups", "row", "chan"), "col", None)
    return jax.shard_map(functools.partial(local_any, axis_sizes), mesh=mesh, in_specs=in_specs, out_specs=out_specs, check_vma=False)
```
